32 devices in a mesh: dp: 8 (over z, x), tensor: 4 (over y, core).
Axes of the slice: x: 2, y: 2, z: 4, core: 2. Of those that a mesh axis runs over, the one named last changes fastest.
Arguments:
- attn_out: bfloat16 [8192, 8192], P('dp', 'tensor'), may hold values from -6 to 6
- out_grad: bfloat16 [8192, 4096], P('dp'), may hold values from -6 to 6
- completion_ids: int32 [8192], P('dp'), may hold values from 0 to 63, never falling along the last dimension, each value on 1 to 256 neighbouring positions
- rewards: float32 [64], replicated, may hold values from -6 to 6
- master: float32 [4096, 8192], P('dp', 'tensor'), may hold values from -0.0625 to 0.0625
- moment_one: float32 [4096, 8192], P('dp', 'tensor'), may hold values from -4 to 4
- moment_two: float32 [4096, 8192], P('dp', 'tensor'), may hold values from 0.05 to 0.5
Outputs:
- new_weights: bfloat16 [4096, 8192], P(None, 'tensor')
- new_one: float32 [4096, 8192], P('dp', 'tensor')
- new_two: float32 [4096, 8192], P('dp', 'tensor')
The draws below stay inside these ranges and needn't reach their ends.
Inputs may be any that keep to these rules, and one draw needn't show every extreme that they name: `completion_ids`: completion numbers never fall along the tokens; every completion has 1 to 256 tokens and one has exactly 256.
All inputs are finite; a program needn't handle non-finite values.
Results may differ from the reference program's by a relative error of at most 0.013.
Values may be sent and summed in bfloat16 or wider, within the bound.
No kernel may reach another device: no remote copies, remote signals or barrier semaphores. Data moves between devices by JAX's collectives and lax.ppermute only.
A program may use at most 192 MiB of HBM per device.

```python
import math
import jax
import jax.numpy as jnp
import numpy as np
from jax import lax

D = 8192
OUT = 4096
TOK_DEV = 1024
MOST_LEN = 256
GROUP = 8
TOKENS = 8192
COMPLETIONS = 64
N_DP = 8


def spiked(entries, key, source, target, shards_of, factor):
    def block_of(position):
        return (jnp.arange(entries.shape[position]) // (entries.shape[position] // shards_of)).reshape((-1,) + (1,) * (entries.ndim - 1 - position))

    one_side = jax.random.permutation(key, shards_of)[block_of(target)]
    other_side = (block_of(target) + shards_of // 2) % shards_of
    return jnp.where((block_of(source) == one_side) | (block_of(source) == other_side), factor * entries, entries)


def block_levels(key, extent, split, low, top_value):
    level, own = 1.0, jax.random.fold_in(key, 6)
    for position, parts in split:
        draws = jnp.exp(jax.random.uniform(jax.random.fold_in(own, position), (parts,), jnp.float32, low / len(split), top_value / len(split)))
        level = level * jnp.repeat(draws, extent[position] // parts).reshape([-1 if axis == position else 1 for axis in range(len(extent))])
    return level


def split_up(amount, total, reach, skew):
    weights = [(1 << 20) // math.isqrt(grade ** skew) + 1 for grade in range(2, amount + 1)]
    surplus, given = total - reach - (amount - 1), [1] * (amount - 1)
    while surplus > 0:
        movable = [i for i in range(amount - 1) if given[i] < reach]
        pool, remaining = sum([weights[i] for i in movable]), surplus
        for i in movable:
            addition = min(reach - given[i], max(1, remaining * weights[i] // pool), surplus)
            given[i] = given[i] + addition
            surplus = surplus - addition
    return np.array([reach] + given)


def uneven_parts(key, count, total, most, slope):
    if count == 2:
        one = jax.random.randint(key, (), max(1, total - most), min(most, total - 1) + 1)
        return jnp.stack([one, total - one])
    sizes = jnp.asarray(split_up(count, total, most, slope), jnp.int32)
    twos = (count - 1) // 2
    giver, receiver = sizes[1:1 + 2 * twos:2], sizes[2:2 + 2 * twos:2]
    margin = jnp.minimum(giver - 1, most - receiver)
    passed = jax.random.randint(jax.random.fold_in(key, 1), (twos,), 0, 1 << 20) % (margin + 1)
    sizes = sizes.at[1:1 + 2 * twos:2].set(giver - passed).at[2:2 + 2 * twos:2].set(receiver + passed)
    return sizes[jax.random.permutation(jax.random.fold_in(key, 2), count)]


def bell_draw(stream_key, dims, scale, bound, pieces=(), held_as=jnp.bfloat16):
    factor_of = block_levels(stream_key, dims, pieces, -0.22, 0.18) if pieces else 1.0
    drawn = jax.random.normal(stream_key, dims, jnp.float32) * scale * factor_of
    return jnp.minimum(jnp.maximum(drawn, -bound), bound).astype(held_as)


def gaussian_with(key, extent, scale, most, shards, heavy, kind=jnp.bfloat16):
    result = scale * jax.random.normal(key, extent, jnp.float32)
    if shards:
        result = result * block_levels(key, extent, shards, -0.22, 0.18)
    return jnp.clip(spiked(result, jax.random.fold_in(key, 3), *heavy), -most, most).astype(kind)


def setup_inputs(seed: int = 0) -> dict:
    splits = jax.random.split(jax.random.key(seed), 8)
    attn_out = bell_draw(splits[0], (TOKENS, D), 1.0, 6.0, ((0, 8), (1, 4)))
    out_grad = gaussian_with(splits[1], (TOKENS, OUT), 1.0, 6.0, ((0, 8),), (0, 1, 8, 2.0))
    completion_ids = jnp.searchsorted(jnp.cumsum(uneven_parts(splits[2], COMPLETIONS, TOKENS, MOST_LEN, 0)), jnp.arange(TOKENS), side="right").astype(jnp.int32)
    rewards = bell_draw(splits[3], (COMPLETIONS,), 1.5, 6.0, (), jnp.float32)
    master = bell_draw(splits[4], (OUT, D), D ** -0.5, 0.0625, ((0, 8), (1, 4)), jnp.float32)
    moment_one = bell_draw(splits[5], (OUT, D), 0.3, 4.0, ((0, 8), (1, 4)), jnp.float32)
    moment_two = jnp.clip(jnp.exp(math.log(0.5) - 2.3025851 * jax.random.uniform(splits[6], (OUT, D), jnp.float32) ** block_levels(splits[6], (OUT, D), ((0, 8), (1, 4)), -0.2, 0.2)), 0.05, 0.5)
    return {"attn_out": attn_out, "out_grad": out_grad, "completion_ids": completion_ids, "rewards": rewards, "master": master, "moment_one": moment_one, "moment_two": moment_two}


beta_one = 0.9
beta_two = 0.95
learn_rate = 0.01
weight_decay = 0.1
epsilon = 1e-08
adam_step = 10.0

def token_weights(completion_ids, rewards):
    onehot = (completion_ids[:, None] == jnp.arange(COMPLETIONS, dtype=jnp.int32)[None, :]).astype(jnp.float32)
    lengths = lax.optimization_barrier(jnp.sum(onehot, axis=0))
    grouped = rewards.reshape(COMPLETIONS // GROUP, GROUP)
    center = lax.optimization_barrier(jnp.mean(grouped, axis=1, keepdims=True))
    spread = jnp.sqrt(lax.optimization_barrier(jnp.mean((grouped - center) * (grouped - center), axis=1, keepdims=True)))
    advantage = ((grouped - center) / jnp.maximum(spread, 1.0)).reshape(-1)
    return jnp.dot(onehot, advantage / lengths, precision=lax.Precision.HIGHEST)

def reference(attn_out, out_grad, completion_ids, rewards, master, moment_one, moment_two):
    token_weight = token_weights(completion_ids, rewards)
    weighted = (out_grad.astype(jnp.float32) * token_weight[:, None]).astype(jnp.bfloat16)
    weighted_blocks = weighted.reshape(N_DP, TOK_DEV, OUT)
    input_blocks = attn_out.reshape(N_DP, TOK_DEV, D)

    def add_block(total, pair):
        partial_value = jnp.dot(pair[0].T, pair[1], preferred_element_type=jnp.float32).astype(jnp.bfloat16)
        partial_value = lax.optimization_barrier(partial_value)
        return (total + partial_value.astype(jnp.float32), None)
    grad, unused = lax.scan(add_block, jnp.zeros((OUT, D), jnp.float32), (weighted_blocks, input_blocks))
    new_one = beta_one * moment_one + (1.0 - beta_one) * grad
    new_two = beta_two * moment_two + (1.0 - beta_two) * grad * grad
    first = new_one / (1.0 - beta_one ** adam_step)
    second = new_two / (1.0 - beta_two ** adam_step)
    update = learn_rate * (first / (jnp.sqrt(second) + epsilon) + weight_decay * master)
    new_weights = (master - update).astype(jnp.bfloat16)
    return (new_weights, new_one, new_two)
```

```python
import collections

import jax
import jax.numpy as jnp
from jax import lax
from jax.experimental.layout import Layout, with_layout_constraint
from jax.sharding import PartitionSpec as P

GROUP = 8
OUTER = 4
CHUNKS = 4
LAG = 2


beta_one = 0.9
beta_two = 0.95
learn_rate = 0.01
weight_decay = 0.1
epsilon = 1e-08
adam_step = 10.0


def token_weights(completion_ids, rewards, count):
    count_all = rewards.shape[0]
    onehot = (completion_ids[:, None] == jnp.arange(count_all, dtype=jnp.int32)[None, :]).astype(
        jnp.float32
    )
    own = jnp.sum(onehot, axis=0)
    before = lax.ppermute(own, "dp", [(d, d + 1) for d in range(count - 1)])
    after = lax.ppermute(own, "dp", [(d + 1, d) for d in range(count - 1)])
    lengths = jnp.maximum(own + before + after, 1.0)
    grouped = rewards.reshape(count_all // GROUP, GROUP)
    center = jnp.mean(grouped, axis=1, keepdims=True)
    spread = jnp.sqrt(jnp.mean((grouped - center) * (grouped - center), axis=1, keepdims=True))
    advantage = ((grouped - center) / jnp.maximum(spread, 1.0)).reshape(-1)
    return jnp.dot(onehot, advantage / lengths, precision=lax.Precision.HIGHEST)


def contract_tokens(left, right):
    return lax.dot_general(
        left, right, (((0,), (0,)), ((), ())), preferred_element_type=jnp.float32
    )


def straight(value):
    return with_layout_constraint(value, Layout(major_to_minor=(0, 1)))


def cycle(count):
    inner = count // OUTER
    walk = [o * inner for o in range(OUTER)]
    for turn, o in enumerate(reversed(range(OUTER))):
        along = range(1, inner) if turn % 2 == 0 else reversed(range(1, inner))
        walk += [o * inner + i for i in along]
    return walk


def shards(attn_out, out_grad, completion_ids, rewards, master, moment_one, moment_two):
    count = lax.psum(1, "dp")
    rows, wide = master.shape
    walk = cycle(count)
    place = [walk.index(d) for d in range(count)]
    me = lax.axis_index("dp")
    table = jnp.asarray(
        [[walk[(place[d] + k) % count] for k in range(count)] for d in range(count)], jnp.int32
    )[me]
    owners = [table[k] for k in range(count)]
    pairs = {
        turn: [(walk[p], walk[(p + turn) % count]) for p in range(count)] for turn in (1, -1)
    }
    token_weight = token_weights(completion_ids, rewards, count)
    part = wide // CHUNKS
    turns = [1 if index % 2 == 0 else -1 for index in range(CHUNKS)]
    cols = [slice(index * part, (index + 1) * part) for index in range(CHUNKS)]
    blocks = {}

    def weighted(k):
        k = k % count
        if k not in blocks:
            grads = lax.dynamic_slice(out_grad, (0, owners[k] * rows), (out_grad.shape[0], rows))
            blocks[k] = lax.optimization_barrier(
                (grads.astype(jnp.float32) * token_weight[:, None]).astype(jnp.bfloat16)
            )
        return blocks[k]

    def term(index, k):
        return contract_tokens(weighted(k), attn_out[:, cols[index]]).astype(jnp.bfloat16)

    moving = [straight(term(c, -turns[c])) for c in range(CHUNKS)]
    for step in range(1, count):
        for c, turn in enumerate(turns):
            arrived = lax.ppermute(moving[c], "dp", pairs[turn])
            moving[c] = arrived.astype(jnp.float32) + term(c, -turn * (step + 1)).astype(
                jnp.float32
            )
            if step < count - 1:
                moving[c] = straight(moving[c].astype(jnp.bfloat16))
    new_weights = jnp.zeros((count * rows, wide), jnp.bfloat16)
    ones, twos = [], []
    for c, grad in enumerate(moving):
        new_one = beta_one * moment_one[:, cols[c]] + (1.0 - beta_one) * grad
        new_two = beta_two * moment_two[:, cols[c]] + (1.0 - beta_two) * grad * grad
        first = new_one / (1.0 - beta_one**adam_step)
        second = new_two / (1.0 - beta_two**adam_step)
        update = learn_rate * (
            first / (jnp.sqrt(second) + epsilon) + weight_decay * master[:, cols[c]]
        )
        moving[c] = straight((master[:, cols[c]] - update).astype(jnp.bfloat16))
        ones.append(new_one)
        twos.append(new_two)
    waiting = collections.deque()

    def put(into):
        c, step, piece = waiting.popleft()
        at = owners[-turns[c] * step % count]
        return lax.dynamic_update_slice(into, piece, (at * rows, c * part))

    for step in range(count):
        for c, turn in enumerate(turns):
            waiting.append((c, step, moving[c]))
            if len(waiting) > LAG:
                new_weights = put(new_weights)
            if step < count - 1:
                moving[c], new_weights = lax.optimization_barrier((moving[c], new_weights))
                moving[c] = lax.ppermute(moving[c], "dp", pairs[turn])
    while waiting:
        new_weights = put(new_weights)
    return (new_weights, jnp.concatenate(ones, axis=1), jnp.concatenate(twos, axis=1))


def solution(mesh):
    return jax.shard_map(
        shards,
        mesh=mesh,
        in_specs=(
            P("dp", "tensor"),
            P("dp", None),
            P("dp"),
            P(),
            P("dp", "tensor"),
            P("dp", "tensor"),
            P("dp", "tensor"),
        ),
        out_specs=(P(None, "tensor"), P("dp", "tensor"), P("dp", "tensor")),
        check_vma=False,
    )
```

```python
import collections

import jax
import jax.numpy as jnp
from jax import lax
from jax.experimental.layout import Layout, with_layout_constraint
from jax.sharding import PartitionSpec as P

GROUP = 8
OUTER = 4
CHUNKS = 4
LAG = 2
AHEAD = 3


beta_one = 0.9
beta_two = 0.95
learn_rate = 0.01
weight_decay = 0.1
epsilon = 1e-08
adam_step = 10.0


def token_weights(completion_ids, rewards, count):
    count_all = rewards.shape[0]
    onehot = (completion_ids[:, None] == jnp.arange(count_all, dtype=jnp.int32)[None, :]).astype(
        jnp.float32
    )
    own = jnp.sum(onehot, axis=0)
    before = lax.ppermute(own, "dp", [(d, d + 1) for d in range(count - 1)])
    after = lax.ppermute(own, "dp", [(d + 1, d) for d in range(count - 1)])
    lengths = jnp.maximum(own + before + after, 1.0)
    grouped = rewards.reshape(count_all // GROUP, GROUP)
    center = jnp.mean(grouped, axis=1, keepdims=True)
    spread = jnp.sqrt(jnp.mean((grouped - center) * (grouped - center), axis=1, keepdims=True))
    advantage = ((grouped - center) / jnp.maximum(spread, 1.0)).reshape(-1)
    return jnp.dot(onehot, advantage / lengths, precision=lax.Precision.HIGHEST)


def contract_tokens(left, right):
    return lax.dot_general(
        left, right, (((0,), (0,)), ((), ())), preferred_element_type=jnp.float32
    )


def straight(value):
    return with_layout_constraint(value, Layout(major_to_minor=(0, 1)))


def cycle(count):
    inner = count // OUTER
    walk = [o * inner for o in range(OUTER)]
    for turn, o in enumerate(reversed(range(OUTER))):
        along = range(1, inner) if turn % 2 == 0 else reversed(range(1, inner))
        walk += [o * inner + i for i in along]
    return walk


def shards(attn_out, out_grad, completion_ids, rewards, master, moment_one, moment_two):
    count = lax.psum(1, "dp")
    rows, wide = master.shape
    walk = cycle(count)
    place = [walk.index(d) for d in range(count)]
    me = lax.axis_index("dp")
    table = jnp.asarray(
        [[walk[(place[d] + k) % count] for k in range(count)] for d in range(count)], jnp.int32
    )[me]
    owners = [table[k] for k in range(count)]
    pairs = {
        turn: [(walk[p], walk[(p + turn) % count]) for p in range(count)] for turn in (1, -1)
    }
    token_weight = token_weights(completion_ids, rewards, count)
    part = wide // CHUNKS
    turns = [1 if index % 2 == 0 else -1 for index in range(CHUNKS)]
    cols = [slice(index * part, (index + 1) * part) for index in range(CHUNKS)]
    blocks = {}

    def weighted(k, gate):
        grads = lax.dynamic_slice(out_grad, (0, owners[k] * rows), (out_grad.shape[0], rows))
        return (grads.astype(jnp.float32) * gate[:, None]).astype(jnp.bfloat16)

    def term(c, step):
        left = blocks[-turns[c] * step % count]
        value = contract_tokens(left, attn_out[:, cols[c]])
        return straight(value.astype(jnp.bfloat16))

    gate = token_weight
    for turn in (1, -1):
        blocks[-turn % count] = weighted(-turn % count, gate)
    moving = []
    for c in range(CHUNKS):
        value, gate = lax.optimization_barrier((term(c, 1), gate))
        moving.append(value)
    events = [(step, c) for step in range(1, count) for c in range(CHUNKS)]
    terms = {}

    def prepare(number, gate):
        if number < len(events):
            step, c = events[number]
            k = -turns[c] * (step + 1) % count
            if k not in blocks:
                blocks[k] = weighted(k, gate)
            blocks[k], gate = lax.optimization_barrier((blocks[k], gate))
            terms[number] = term(c, step + 1)
        return gate

    for number, (step, c) in enumerate(events):
        arrived = lax.ppermute(moving[c], "dp", pairs[turns[c]])
        if number == 0:
            gate = prepare(0, gate)
        arrived, gate = lax.optimization_barrier((arrived, gate))
        if number == 0:
            for early in range(1, AHEAD):
                gate = prepare(early, gate)
        moving[c] = arrived.astype(jnp.float32) + terms.pop(number).astype(jnp.float32)
        if step < count - 1:
            moving[c] = straight(moving[c].astype(jnp.bfloat16))
        moving[c], gate = lax.optimization_barrier((moving[c], gate))
        gate = prepare(number + AHEAD, gate)
    new_weights = jnp.zeros((count * rows, wide), jnp.bfloat16)
    ones, twos = [], []
    for c in range(CHUNKS):
        grad = moving[c]
        if c:
            grad, moving[c - 1] = lax.optimization_barrier((grad, moving[c - 1]))
        new_one = beta_one * moment_one[:, cols[c]] + (1.0 - beta_one) * grad
        new_two = beta_two * moment_two[:, cols[c]] + (1.0 - beta_two) * grad * grad
        first = new_one / (1.0 - beta_one**adam_step)
        second = new_two / (1.0 - beta_two**adam_step)
        update = learn_rate * (
            first / (jnp.sqrt(second) + epsilon) + weight_decay * master[:, cols[c]]
        )
        moving[c] = straight((master[:, cols[c]] - update).astype(jnp.bfloat16))
        ones.append(new_one)
        twos.append(new_two)
    new_one, new_two = jnp.concatenate(ones, axis=1), jnp.concatenate(twos, axis=1)
    waiting = collections.deque()

    def put(into):
        c, step, piece = waiting.popleft()
        at = owners[-turns[c] * step % count]
        return lax.dynamic_update_slice(into, piece, (at * rows, c * part))

    for step in range(count):
        if step == 3:
            new_weights, new_one, new_two = lax.optimization_barrier(
                (new_weights, new_one, new_two)
            )
        for c, turn in enumerate(turns):
            waiting.append((c, step, moving[c]))
            if len(waiting) > LAG:
                new_weights = put(new_weights)
            if step < count - 1:
                moving[c], new_weights = lax.optimization_barrier((moving[c], new_weights))
                moving[c] = lax.ppermute(moving[c], "dp", pairs[turn])
    while waiting:
        new_weights = put(new_weights)
    return (new_weights, new_one, new_two)


def solution(mesh):
    return jax.shard_map(
        shards,
        mesh=mesh,
        in_specs=(
            P("dp", "tensor"),
            P("dp", None),
            P("dp"),
            P(),
            P("dp", "tensor"),
            P("dp", "tensor"),
            P("dp", "tensor"),
        ),
        out_specs=(P(None, "tensor"), P("dp", "tensor"), P("dp", "tensor")),
        check_vma=False,
    )
```

```python
import collections

import jax
import jax.numpy as jnp
from jax import lax
from jax.experimental import pallas as pl
from jax.experimental.pallas import tpu as pltpu
from jax.experimental.layout import Layout, with_layout_constraint
from jax.sharding import PartitionSpec as P

GROUP = 8
OUTER = 4
CHUNKS = 4
LAG = 2
HOIST = 28
SPREAD = (1, 2, 3, 4)
FREE = 1
AHEAD = 3


beta_one = 0.9
beta_two = 0.95
learn_rate = 0.01
weight_decay = 0.1
epsilon = 1e-08
adam_step = 10.0


def token_weights(completion_ids, rewards, count):
    count_all = rewards.shape[0]
    onehot = (completion_ids[:, None] == jnp.arange(count_all, dtype=jnp.int32)[None, :]).astype(
        jnp.float32
    )
    own = jnp.sum(onehot, axis=0)
    before = lax.ppermute(own, "dp", [(d, d + 1) for d in range(count - 1)])
    after = lax.ppermute(own, "dp", [(d + 1, d) for d in range(count - 1)])
    lengths = jnp.maximum(own + before + after, 1.0)
    grouped = rewards.reshape(count_all // GROUP, GROUP)
    center = jnp.mean(grouped, axis=1, keepdims=True)
    spread = jnp.sqrt(jnp.mean((grouped - center) * (grouped - center), axis=1, keepdims=True))
    advantage = ((grouped - center) / jnp.maximum(spread, 1.0)).reshape(-1)
    return jnp.dot(onehot, advantage / lengths, precision=lax.Precision.HIGHEST)


def contract_tokens(left, right):
    return lax.dot_general(
        left, right, (((0,), (0,)), ((), ())), preferred_element_type=jnp.float32
    )


def straight(value):
    return with_layout_constraint(value, Layout(major_to_minor=(0, 1)))


def place(whole, piece, row, column):
    shape, in_place = whole.shape, not isinstance(whole, jax.ShapeDtypeStruct)

    def body(row_ref, piece_ref, *rest):
        whole_ref, sem = rest[-2:]
        first = pl.multiple_of(row_ref[0], piece.shape[0])
        copy = pltpu.make_async_copy(
            piece_ref,
            whole_ref.at[pl.ds(first, piece.shape[0]), pl.ds(column, piece.shape[1])],
            sem,
        )
        copy.start()
        copy.wait()

    return pl.pallas_call(
        body,
        out_shape=jax.ShapeDtypeStruct(shape, whole.dtype),
        grid_spec=pltpu.PrefetchScalarGridSpec(
            num_scalar_prefetch=1,
            grid=(1,),
            in_specs=[pl.BlockSpec(memory_space=pl.ANY)]
            + [pl.BlockSpec(memory_space=pltpu.HBM)] * in_place,
            out_specs=pl.BlockSpec(memory_space=pltpu.HBM),
            scratch_shapes=[pltpu.SemaphoreType.DMA],
        ),
        input_output_aliases={2: 0} if in_place else {},
        compiler_params=pltpu.CompilerParams(vmem_limit_bytes=1 << 20),
        cost_estimate=pl.CostEstimate(flops=0, bytes_accessed=1024, transcendentals=0),
    )(row.reshape(1), piece, *([whole] if in_place else []))


def cycle(count):
    inner = count // OUTER
    walk = [o * inner for o in range(OUTER)]
    for turn, o in enumerate(reversed(range(OUTER))):
        along = range(1, inner) if turn % 2 == 0 else reversed(range(1, inner))
        walk += [o * inner + i for i in along]
    return walk


def shards(attn_out, out_grad, completion_ids, rewards, master, moment_one, moment_two):
    count = lax.psum(1, "dp")
    rows, wide = master.shape
    walk = cycle(count)
    places = [walk.index(d) for d in range(count)]
    me = lax.axis_index("dp")
    table = jnp.asarray(
        [[walk[(places[d] + k) % count] for k in range(count)] for d in range(count)], jnp.int32
    )[me]
    owners = [table[k] for k in range(count)]
    pairs = {
        turn: [(walk[p], walk[(p + turn) % count]) for p in range(count)] for turn in (1, -1)
    }
    token_weight = token_weights(completion_ids, rewards, count)
    part = wide // CHUNKS
    turns = [1 if index % 2 == 0 else -1 for index in range(CHUNKS)]
    cols = [slice(index * part, (index + 1) * part) for index in range(CHUNKS)]
    blocks = {}

    def weighted(k, gate):
        grads = lax.dynamic_slice(out_grad, (0, owners[k] * rows), (out_grad.shape[0], rows))
        return (grads.astype(jnp.float32) * gate[:, None]).astype(jnp.bfloat16)

    def term(c, step):
        left = blocks[-turns[c] * step % count]
        value = contract_tokens(left, attn_out[:, cols[c]])
        return straight(value.astype(jnp.bfloat16))

    gate = token_weight
    for turn in (1, -1):
        blocks[-turn % count] = weighted(-turn % count, gate)
    moving = []
    for c in range(CHUNKS):
        value, gate = lax.optimization_barrier((term(c, 1), gate))
        moving.append(value)
    events = [(step, c) for step in range(1, count) for c in range(CHUNKS)]
    terms = {}

    def prepare(number, gate):
        if number < len(events):
            step, c = events[number]
            k = -turns[c] * (step + 1) % count
            if k not in blocks:
                blocks[k] = weighted(k, gate)
            blocks[k], gate = lax.optimization_barrier((blocks[k], gate))
            terms[number] = term(c, step + 1)
        return gate

    for number, (step, c) in enumerate(events):
        arrived = lax.ppermute(moving[c], "dp", pairs[turns[c]])
        if number == 0:
            gate = prepare(0, gate)
        if number < FREE:
            arrived, gate = lax.optimization_barrier((arrived, gate))
        if number == 0:
            for early in range(1, HOIST):
                gate = prepare(early, gate)
        moving[c] = arrived.astype(jnp.float32) + terms.pop(number).astype(jnp.float32)
        if step < count - 1:
            moving[c] = straight(moving[c].astype(jnp.bfloat16))
        if number < FREE:
            moving[c], gate = lax.optimization_barrier((moving[c], gate))
        while len(terms) + number + 1 < min(max(HOIST, number + 1 + AHEAD), len(events)):
            gate = prepare(len(terms) + number + 1, gate)
    new_weights = jax.ShapeDtypeStruct((count * rows, wide), jnp.bfloat16)
    new_one = new_two = jax.ShapeDtypeStruct((rows, wide), jnp.float32)
    top = jnp.zeros((), jnp.int32)
    ones, twos = [], []
    for c in range(CHUNKS):
        grad = moving[c]
        if c:
            grad, moving[c - 1] = lax.optimization_barrier((grad, moving[c - 1]))
        one = beta_one * moment_one[:, cols[c]] + (1.0 - beta_one) * grad
        two = beta_two * moment_two[:, cols[c]] + (1.0 - beta_two) * grad * grad
        first = one / (1.0 - beta_one**adam_step)
        second = two / (1.0 - beta_two**adam_step)
        update = learn_rate * (
            first / (jnp.sqrt(second) + epsilon) + weight_decay * master[:, cols[c]]
        )
        moving[c] = straight((master[:, cols[c]] - update).astype(jnp.bfloat16))
        ones.append(straight(one))
        twos.append(straight(two))
    waiting = collections.deque()

    def put(into):
        c, step, piece = waiting.popleft()
        at = owners[-turns[c] * step % count]
        return place(into, piece, at * rows, c * part)

    for step in range(count):
        for c, turn in enumerate(turns):
            waiting.append((c, step, moving[c]))
            if len(waiting) > LAG:
                new_weights = put(new_weights)
            if step < count - 1:
                if step or c >= LAG:
                    moving[c], new_weights = lax.optimization_barrier((moving[c], new_weights))
                moving[c] = lax.ppermute(moving[c], "dp", pairs[turn])
        for c in range(CHUNKS):
            if SPREAD[c] == step:
                new_one = place(new_one, ones[c], top, c * part)
                new_two = place(new_two, twos[c], top, c * part)
                new_weights, new_one, new_two = lax.optimization_barrier(
                    (new_weights, new_one, new_two)
                )
    while waiting:
        new_weights = put(new_weights)
    return (new_weights, new_one, new_two)


def solution(mesh):
    return jax.shard_map(
        shards,
        mesh=mesh,
        in_specs=(
            P("dp", "tensor"),
            P("dp", None),
            P("dp"),
            P(),
            P("dp", "tensor"),
            P("dp", "tensor"),
            P("dp", "tensor"),
        ),
        out_specs=(P(None, "tensor"), P("dp", "tensor"), P("dp", "tensor")),
        check_vma=False,
    )
```

```python
import collections

import jax
import jax.numpy as jnp
from jax import lax
from jax.experimental import pallas as pl
from jax.experimental.pallas import tpu as pltpu
from jax.experimental.layout import Layout, with_layout_constraint
from jax.sharding import PartitionSpec as P

GROUP = 8
OUTER = 4
CHUNKS = 4
LAG = 2
HOIST = 28
SPREAD = (1, 2, 3, 4)
FREE = 1
AHEAD = 3


beta_one = 0.9
beta_two = 0.95
learn_rate = 0.01
weight_decay = 0.1
epsilon = 1e-08
adam_step = 10.0


def token_weights(completion_ids, rewards, count):
    count_all = rewards.shape[0]
    onehot = (completion_ids[:, None] == jnp.arange(count_all, dtype=jnp.int32)[None, :]).astype(
        jnp.float32
    )
    own = jnp.sum(onehot, axis=0)
    before = lax.ppermute(own, "dp", [(d, d ^ 1) for d in range(count)])
    after = lax.ppermute(
        own, "dp", [(d, d - 1 + 2 * (d % 2)) for d in range(1, count - 1)]
    )
    lengths = jnp.maximum(own + before + after, 1.0)
    grouped = rewards.reshape(count_all // GROUP, GROUP)
    center = jnp.mean(grouped, axis=1, keepdims=True)
    spread = jnp.sqrt(jnp.mean((grouped - center) * (grouped - center), axis=1, keepdims=True))
    advantage = ((grouped - center) / jnp.maximum(spread, 1.0)).reshape(-1)
    return jnp.dot(onehot, advantage / lengths, precision=lax.Precision.HIGHEST)


def contract_tokens(left, right):
    return lax.dot_general(
        left, right, (((0,), (0,)), ((), ())), preferred_element_type=jnp.float32
    )


def straight(value):
    return with_layout_constraint(value, Layout(major_to_minor=(0, 1)))


def place(whole, piece, row, column):
    shape, in_place = whole.shape, not isinstance(whole, jax.ShapeDtypeStruct)

    def body(row_ref, piece_ref, *rest):
        whole_ref, sem = rest[-2:]
        first = pl.multiple_of(row_ref[0], piece.shape[0])
        copy = pltpu.make_async_copy(
            piece_ref,
            whole_ref.at[pl.ds(first, piece.shape[0]), pl.ds(column, piece.shape[1])],
            sem,
        )
        copy.start()
        copy.wait()

    return pl.pallas_call(
        body,
        out_shape=jax.ShapeDtypeStruct(shape, whole.dtype),
        grid_spec=pltpu.PrefetchScalarGridSpec(
            num_scalar_prefetch=1,
            grid=(1,),
            in_specs=[pl.BlockSpec(memory_space=pl.ANY)]
            + [pl.BlockSpec(memory_space=pltpu.HBM)] * in_place,
            out_specs=pl.BlockSpec(memory_space=pltpu.HBM),
            scratch_shapes=[pltpu.SemaphoreType.DMA],
        ),
        input_output_aliases={2: 0} if in_place else {},
        compiler_params=pltpu.CompilerParams(vmem_limit_bytes=1 << 20),
        cost_estimate=pl.CostEstimate(flops=0, bytes_accessed=1024, transcendentals=0),
    )(row.reshape(1), piece, *([whole] if in_place else []))


def cycle(count):
    inner = count // OUTER
    walk = [o * inner for o in range(OUTER)]
    for turn, o in enumerate(reversed(range(OUTER))):
        along = range(1, inner) if turn % 2 == 0 else reversed(range(1, inner))
        walk += [o * inner + i for i in along]
    return walk


def place_of(d, count):
    inner = count // OUTER
    o, i = lax.div(d, inner), lax.rem(d, inner)
    turn = OUTER - 1 - o
    along = jnp.where(lax.rem(turn, 2) == 0, i - 1, inner - 1 - i)
    return jnp.where(i == 0, o, OUTER + turn * (inner - 1) + along)


def at_place(p, count):
    inner = count // OUTER
    q = jnp.maximum(p - OUTER, 0)
    turn, along = lax.div(q, inner - 1), lax.rem(q, inner - 1)
    i = jnp.where(lax.rem(turn, 2) == 0, 1 + along, inner - 1 - along)
    return jnp.where(p < OUTER, p * inner, (OUTER - 1 - turn) * inner + i)


def shards(attn_out, out_grad, completion_ids, rewards, master, moment_one, moment_two):
    count = lax.psum(1, "dp")
    rows, wide = master.shape
    walk = cycle(count)
    me = lax.axis_index("dp")
    here = place_of(me, count)
    owners = [at_place(lax.rem(here + k, count), count) for k in range(count)]
    pairs = {
        turn: [(walk[p], walk[(p + turn) % count]) for p in range(count)] for turn in (1, -1)
    }
    token_weight = token_weights(completion_ids, rewards, count)
    part = wide // CHUNKS
    turns = [1 if index % 2 == 0 else -1 for index in range(CHUNKS)]
    cols = [slice(index * part, (index + 1) * part) for index in range(CHUNKS)]
    blocks = {}

    def weighted(k, gate):
        grads = lax.dynamic_slice(out_grad, (0, owners[k] * rows), (out_grad.shape[0], rows))
        return (grads.astype(jnp.float32) * gate[:, None]).astype(jnp.bfloat16)

    def term(c, step):
        left = blocks[-turns[c] * step % count]
        value = contract_tokens(left, attn_out[:, cols[c]])
        return straight(value.astype(jnp.bfloat16))

    gate = token_weight
    for turn in (1, -1):
        blocks[-turn % count] = weighted(-turn % count, gate)
    moving = []
    for c in range(CHUNKS):
        value, gate = lax.optimization_barrier((term(c, 1), gate))
        moving.append(value)
    events = [(step, c) for step in range(1, count) for c in range(CHUNKS)]
    terms = {}

    def prepare(number, gate):
        if number < len(events):
            step, c = events[number]
            k = -turns[c] * (step + 1) % count
            if k not in blocks:
                blocks[k] = weighted(k, gate)
            blocks[k], gate = lax.optimization_barrier((blocks[k], gate))
            terms[number] = term(c, step + 1)
        return gate

    for number, (step, c) in enumerate(events):
        arrived = lax.ppermute(moving[c], "dp", pairs[turns[c]])
        if number == 0:
            gate = prepare(0, gate)
        if number < FREE:
            arrived, gate = lax.optimization_barrier((arrived, gate))
        if number == 0:
            for early in range(1, HOIST):
                gate = prepare(early, gate)
        moving[c] = arrived.astype(jnp.float32) + terms.pop(number).astype(jnp.float32)
        if step < count - 1:
            moving[c] = straight(moving[c].astype(jnp.bfloat16))
        if number < FREE:
            moving[c], gate = lax.optimization_barrier((moving[c], gate))
        while len(terms) + number + 1 < min(max(HOIST, number + 1 + AHEAD), len(events)):
            gate = prepare(len(terms) + number + 1, gate)
    new_weights = jax.ShapeDtypeStruct((count * rows, wide), jnp.bfloat16)
    new_one = new_two = jax.ShapeDtypeStruct((rows, wide), jnp.float32)
    top = jnp.zeros((), jnp.int32)
    ones, twos = [], []
    for c in range(CHUNKS):
        grad = moving[c]
        if c:
            grad, moving[c - 1] = lax.optimization_barrier((grad, moving[c - 1]))
        one = beta_one * moment_one[:, cols[c]] + (1.0 - beta_one) * grad
        two = beta_two * moment_two[:, cols[c]] + (1.0 - beta_two) * grad * grad
        first = one / (1.0 - beta_one**adam_step)
        second = two / (1.0 - beta_two**adam_step)
        update = learn_rate * (
            first / (jnp.sqrt(second) + epsilon) + weight_decay * master[:, cols[c]]
        )
        moving[c] = straight((master[:, cols[c]] - update).astype(jnp.bfloat16))
        ones.append(straight(one))
        twos.append(straight(two))
    waiting = collections.deque()

    def put(into):
        c, step, piece = waiting.popleft()
        at = owners[-turns[c] * step % count]
        return place(into, piece, at * rows, c * part)

    for step in range(count):
        for c, turn in enumerate(turns):
            waiting.append((c, step, moving[c]))
            if len(waiting) > LAG:
                new_weights = put(new_weights)
            if step < count - 1:
                if step or c >= LAG:
                    moving[c], new_weights = lax.optimization_barrier((moving[c], new_weights))
                moving[c] = lax.ppermute(moving[c], "dp", pairs[turn])
        for c in range(CHUNKS):
            if SPREAD[c] == step:
                new_one = place(new_one, ones[c], top, c * part)
                new_two = place(new_two, twos[c], top, c * part)
                new_weights, new_one, new_two = lax.optimization_barrier(
                    (new_weights, new_one, new_two)
                )
    while waiting:
        new_weights = put(new_weights)
    return (new_weights, new_one, new_two)


def solution(mesh):
    return jax.shard_map(
        shards,
        mesh=mesh,
        in_specs=(
            P("dp", "tensor"),
            P("dp", None),
            P("dp"),
            P(),
            P("dp", "tensor"),
            P("dp", "tensor"),
            P("dp", "tensor"),
        ),
        out_specs=(P(None, "tensor"), P("dp", "tensor"), P("dp", "tensor")),
        check_vma=False,
    )
```

```python
import collections

import jax
import jax.numpy as jnp
from jax import lax
from jax.experimental import pallas as pl
from jax.experimental.pallas import tpu as pltpu
from jax.experimental.layout import Layout, with_layout_constraint
from jax.sharding import PartitionSpec as P

GROUP = 8
OUTER = 4
CHUNKS = 4
LAG = 2
FIRST = 16
SPREAD = (1, 2, 3, 4)
FREE = 2


beta_one = 0.9
beta_two = 0.95
learn_rate = 0.01
weight_decay = 0.1
epsilon = 1e-08
adam_step = 10.0


def token_weights(completion_ids, rewards, count):
    count_all = rewards.shape[0]
    onehot = (completion_ids[:, None] == jnp.arange(count_all, dtype=jnp.int32)[None, :]).astype(
        jnp.float32
    )
    own = jnp.sum(onehot, axis=0)
    before = lax.ppermute(own, "dp", [(d, d ^ 1) for d in range(count)])
    after = lax.ppermute(
        own, "dp", [(d, d - 1 + 2 * (d % 2)) for d in range(1, count - 1)]
    )
    lengths = jnp.maximum(own + before + after, 1.0)
    grouped = rewards.reshape(count_all // GROUP, GROUP)
    center = jnp.mean(grouped, axis=1, keepdims=True)
    spread = jnp.sqrt(jnp.mean((grouped - center) * (grouped - center), axis=1, keepdims=True))
    advantage = ((grouped - center) / jnp.maximum(spread, 1.0)).reshape(-1)
    return jnp.dot(onehot, advantage / lengths, precision=lax.Precision.HIGHEST)


def contract_tokens(left, right):
    return lax.dot_general(
        left, right, (((0,), (0,)), ((), ())), preferred_element_type=jnp.float32
    )


def straight(value):
    return with_layout_constraint(value, Layout(major_to_minor=(0, 1)))


def place(whole, piece, row, column):
    shape, in_place = whole.shape, not isinstance(whole, jax.ShapeDtypeStruct)

    def body(row_ref, piece_ref, *rest):
        whole_ref, sem = rest[-2:]
        first = pl.multiple_of(row_ref[0], piece.shape[0])
        copy = pltpu.make_async_copy(
            piece_ref,
            whole_ref.at[pl.ds(first, piece.shape[0]), pl.ds(column, piece.shape[1])],
            sem,
        )
        copy.start()
        copy.wait()

    return pl.pallas_call(
        body,
        out_shape=jax.ShapeDtypeStruct(shape, whole.dtype),
        grid_spec=pltpu.PrefetchScalarGridSpec(
            num_scalar_prefetch=1,
            grid=(1,),
            in_specs=[pl.BlockSpec(memory_space=pl.ANY)]
            + [pl.BlockSpec(memory_space=pltpu.HBM)] * in_place,
            out_specs=pl.BlockSpec(memory_space=pltpu.HBM),
            scratch_shapes=[pltpu.SemaphoreType.DMA],
        ),
        input_output_aliases={2: 0} if in_place else {},
        compiler_params=pltpu.CompilerParams(vmem_limit_bytes=1 << 20),
        cost_estimate=pl.CostEstimate(flops=0, bytes_accessed=1024, transcendentals=0),
    )(row.reshape(1), piece, *([whole] if in_place else []))


def cycle(count):
    inner = count // OUTER
    walk = [o * inner for o in range(OUTER)]
    for turn, o in enumerate(reversed(range(OUTER))):
        along = range(1, inner) if turn % 2 == 0 else reversed(range(1, inner))
        walk += [o * inner + i for i in along]
    return walk


def place_of(d, count):
    inner = count // OUTER
    o, i = lax.div(d, inner), lax.rem(d, inner)
    turn = OUTER - 1 - o
    along = jnp.where(lax.rem(turn, 2) == 0, i - 1, inner - 1 - i)
    return jnp.where(i == 0, o, OUTER + turn * (inner - 1) + along)


def at_place(p, count):
    inner = count // OUTER
    q = jnp.maximum(p - OUTER, 0)
    turn, along = lax.div(q, inner - 1), lax.rem(q, inner - 1)
    i = jnp.where(lax.rem(turn, 2) == 0, 1 + along, inner - 1 - along)
    return jnp.where(p < OUTER, p * inner, (OUTER - 1 - turn) * inner + i)


def shards(attn_out, out_grad, completion_ids, rewards, master, moment_one, moment_two):
    count = lax.psum(1, "dp")
    rows, wide = master.shape
    walk = cycle(count)
    me = lax.axis_index("dp")
    here = place_of(me, count)
    owners = [at_place(lax.rem(here + k, count), count) for k in range(count)]
    pairs = {
        turn: [(walk[p], walk[(p + turn) % count]) for p in range(count)] for turn in (1, -1)
    }
    token_weight = token_weights(completion_ids, rewards, count)
    part = wide // CHUNKS
    turns = [1 if index % 2 == 0 else -1 for index in range(CHUNKS)]
    half = wide // 2
    starts = [half * (index % 2) + part * (index // 2) for index in range(CHUNKS)]
    cols = [slice(start, start + part) for start in starts]
    blocks = {}

    def weighted(k, gate):
        grads = lax.dynamic_slice(out_grad, (0, owners[k] * rows), (out_grad.shape[0], rows))
        return (grads.astype(jnp.float32) * gate[:, None]).astype(jnp.bfloat16)

    def term(c, step):
        left = blocks[-turns[c] * step % count]
        value = contract_tokens(left, attn_out[:, cols[c]])
        return straight(value.astype(jnp.bfloat16))

    gate = token_weight
    for turn in (1, -1):
        blocks[-turn % count] = weighted(-turn % count, gate)
    moving = []
    for c in range(CHUNKS):
        value, gate = lax.optimization_barrier((term(c, 1), gate))
        moving.append(value)
    events = [(step, c) for step in range(1, count) for c in range(CHUNKS)]
    terms = {}

    def prepare(number, gate):
        if number < len(events):
            step, c = events[number]
            k = -turns[c] * (step + 1) % count
            if k not in blocks:
                blocks[k] = weighted(k, gate)
            blocks[k], gate = lax.optimization_barrier((blocks[k], gate))
            terms[number] = term(c, step + 1)
        return gate

    gate = prepare(0, gate)
    ready = 1
    for number, (step, c) in enumerate(events):
        arrived = lax.ppermute(moving[c], "dp", pairs[turns[c]])
        if number < FREE:
            arrived, gate = lax.optimization_barrier((arrived, gate))
        if number == 0:
            while ready < min(FIRST, len(events)):
                gate = prepare(ready, gate)
                ready += 1
        moving[c] = arrived.astype(jnp.float32) + terms.pop(number).astype(jnp.float32)
        if step < count - 1:
            moving[c] = straight(moving[c].astype(jnp.bfloat16))
        if number < FREE:
            moving[c], gate = lax.optimization_barrier((moving[c], gate))
        while number == FREE - 1 and ready < len(events):
            gate = prepare(ready, gate)
            ready += 1
    new_weights = jax.ShapeDtypeStruct((count * rows, wide), jnp.bfloat16)
    new_one = new_two = jax.ShapeDtypeStruct((rows, wide), jnp.float32)
    top = jnp.zeros((), jnp.int32)
    ones, twos = [], []
    for c in range(CHUNKS):
        grad = moving[c]
        if c:
            grad, moving[c - 1] = lax.optimization_barrier((grad, moving[c - 1]))
        one = beta_one * moment_one[:, cols[c]] + (1.0 - beta_one) * grad
        two = beta_two * moment_two[:, cols[c]] + (1.0 - beta_two) * grad * grad
        first = one / (1.0 - beta_one**adam_step)
        second = two / (1.0 - beta_two**adam_step)
        update = learn_rate * (
            first / (jnp.sqrt(second) + epsilon) + weight_decay * master[:, cols[c]]
        )
        moving[c] = straight((master[:, cols[c]] - update).astype(jnp.bfloat16))
        ones.append(straight(one))
        twos.append(straight(two))
    waiting = collections.deque()

    def put(into):
        c, step, piece = waiting.popleft()
        at = owners[-turns[c] * step % count]
        return place(into, piece, at * rows, starts[c])

    for step in range(count):
        for c, turn in enumerate(turns):
            waiting.append((c, step, moving[c]))
            if len(waiting) > LAG:
                new_weights = put(new_weights)
            if step < count - 1:
                if step or c >= LAG:
                    moving[c], new_weights = lax.optimization_barrier((moving[c], new_weights))
                moving[c] = lax.ppermute(moving[c], "dp", pairs[turn])
        for c in range(CHUNKS):
            if SPREAD[c] == step:
                new_one = place(new_one, ones[c], top, starts[c])
                new_two = place(new_two, twos[c], top, starts[c])
                new_weights, new_one, new_two = lax.optimization_barrier(
                    (new_weights, new_one, new_two)
                )
    while waiting:
        new_weights = put(new_weights)
    return (new_weights, new_one, new_two)


def solution(mesh):
    return jax.shard_map(
        shards,
        mesh=mesh,
        in_specs=(
            P("dp", "tensor"),
            P("dp", None),
            P("dp"),
            P(),
            P("dp", "tensor"),
            P("dp", "tensor"),
            P("dp", "tensor"),
        ),
        out_specs=(P(None, "tensor"), P("dp", "tensor"), P("dp", "tensor")),
        check_vma=False,
    )
```

```python
import collections

import jax
import jax.numpy as jnp
from jax import lax
from jax.experimental import pallas as pl
from jax.experimental.pallas import tpu as pltpu
from jax.experimental.layout import Layout, with_layout_constraint
from jax.sharding import PartitionSpec as P

GROUP = 8
OUTER = 4
CHUNKS = 4
LAG = 2
FIRST = 12
SECOND = 20
SPREAD = (1, 2, 3, 4)
FREE = 2


beta_one = 0.9
beta_two = 0.95
learn_rate = 0.01
weight_decay = 0.1
epsilon = 1e-08
adam_step = 10.0


def token_weights(completion_ids, rewards, count):
    count_all = rewards.shape[0]
    onehot = (completion_ids[:, None] == jnp.arange(count_all, dtype=jnp.int32)[None, :]).astype(
        jnp.float32
    )
    own = jnp.sum(onehot, axis=0)
    before = lax.ppermute(own, "dp", [(d, d ^ 1) for d in range(count)])
    after = lax.ppermute(
        own, "dp", [(d, d - 1 + 2 * (d % 2)) for d in range(1, count - 1)]
    )
    lengths = jnp.maximum(own + before + after, 1.0)
    grouped = rewards.reshape(count_all // GROUP, GROUP)
    center = jnp.mean(grouped, axis=1, keepdims=True)
    spread = jnp.sqrt(jnp.mean((grouped - center) * (grouped - center), axis=1, keepdims=True))
    advantage = ((grouped - center) / jnp.maximum(spread, 1.0)).reshape(-1)
    return jnp.dot(onehot, advantage / lengths, precision=lax.Precision.HIGHEST)


def contract_tokens(left, right):
    return lax.dot_general(
        left, right, (((0,), (0,)), ((), ())), preferred_element_type=jnp.float32
    )


def straight(value):
    return with_layout_constraint(value, Layout(major_to_minor=(0, 1)))


def place(whole, piece, row, column):
    shape, in_place = whole.shape, not isinstance(whole, jax.ShapeDtypeStruct)

    def body(row_ref, piece_ref, *rest):
        whole_ref, sem = rest[-2:]
        first = pl.multiple_of(row_ref[0], piece.shape[0])
        copy = pltpu.make_async_copy(
            piece_ref,
            whole_ref.at[pl.ds(first, piece.shape[0]), pl.ds(column, piece.shape[1])],
            sem,
        )
        copy.start()
        copy.wait()

    return pl.pallas_call(
        body,
        out_shape=jax.ShapeDtypeStruct(shape, whole.dtype),
        grid_spec=pltpu.PrefetchScalarGridSpec(
            num_scalar_prefetch=1,
            grid=(1,),
            in_specs=[pl.BlockSpec(memory_space=pl.ANY)]
            + [pl.BlockSpec(memory_space=pltpu.HBM)] * in_place,
            out_specs=pl.BlockSpec(memory_space=pltpu.HBM),
            scratch_shapes=[pltpu.SemaphoreType.DMA],
        ),
        input_output_aliases={2: 0} if in_place else {},
        compiler_params=pltpu.CompilerParams(vmem_limit_bytes=1 << 20),
        cost_estimate=pl.CostEstimate(flops=0, bytes_accessed=1 << 20, transcendentals=0),
    )(row.reshape(1), piece, *([whole] if in_place else []))


def cycle(count):
    inner = count // OUTER
    walk = [o * inner for o in range(OUTER)]
    for turn, o in enumerate(reversed(range(OUTER))):
        along = range(1, inner) if turn % 2 == 0 else reversed(range(1, inner))
        walk += [o * inner + i for i in along]
    return walk


def place_of(d, count):
    inner = count // OUTER
    o, i = lax.div(d, inner), lax.rem(d, inner)
    turn = OUTER - 1 - o
    along = jnp.where(lax.rem(turn, 2) == 0, i - 1, inner - 1 - i)
    return jnp.where(i == 0, o, OUTER + turn * (inner - 1) + along)


def at_place(p, count):
    inner = count // OUTER
    q = jnp.maximum(p - OUTER, 0)
    turn, along = lax.div(q, inner - 1), lax.rem(q, inner - 1)
    i = jnp.where(lax.rem(turn, 2) == 0, 1 + along, inner - 1 - along)
    return jnp.where(p < OUTER, p * inner, (OUTER - 1 - turn) * inner + i)


def shards(attn_out, out_grad, completion_ids, rewards, master, moment_one, moment_two):
    count = lax.psum(1, "dp")
    rows, wide = master.shape
    walk = cycle(count)
    me = lax.axis_index("dp")
    here = place_of(me, count)
    owners = [at_place(lax.rem(here + k, count), count) for k in range(count)]
    pairs = {
        turn: [(walk[p], walk[(p + turn) % count]) for p in range(count)] for turn in (1, -1)
    }
    token_weight = token_weights(completion_ids, rewards, count)
    part = wide // CHUNKS
    turns = [1 if index % 2 == 0 else -1 for index in range(CHUNKS)]
    half = wide // 2
    starts = [half * (index % 2) + part * (index // 2) for index in range(CHUNKS)]
    cols = [slice(start, start + part) for start in starts]
    blocks = {}

    def weighted(k, gate):
        grads = lax.dynamic_slice(out_grad, (0, owners[k] * rows), (out_grad.shape[0], rows))
        return (grads.astype(jnp.float32) * gate[:, None]).astype(jnp.bfloat16)

    def term(c, step):
        left = blocks[-turns[c] * step % count]
        value = contract_tokens(left, attn_out[:, cols[c]])
        return straight(value.astype(jnp.bfloat16))

    gate = token_weight
    for turn in (1, -1):
        blocks[-turn % count] = weighted(-turn % count, gate)
    moving = []
    for c in range(CHUNKS):
        value, gate = lax.optimization_barrier((term(c, 1), gate))
        moving.append(value)
    events = [(step, c) for step in range(1, count) for c in range(CHUNKS)]
    terms = {}

    def prepare(number, gate):
        if number < len(events):
            step, c = events[number]
            k = -turns[c] * (step + 1) % count
            if k not in blocks:
                blocks[k] = weighted(k, gate)
            blocks[k], gate = lax.optimization_barrier((blocks[k], gate))
            terms[number] = term(c, step + 1)
        return gate

    gate = prepare(0, gate)
    ready = 1
    for number, (step, c) in enumerate(events):
        arrived = lax.ppermute(moving[c], "dp", pairs[turns[c]])
        if number < FREE:
            arrived, gate = lax.optimization_barrier((arrived, gate))
        if number == 0:
            while ready < min(FIRST, len(events)):
                gate = prepare(ready, gate)
                ready += 1
        moving[c] = arrived.astype(jnp.float32) + terms.pop(number).astype(jnp.float32)
        if step < count - 1:
            moving[c] = straight(moving[c].astype(jnp.bfloat16))
        if number < FREE:
            moving[c], gate = lax.optimization_barrier((moving[c], gate))
        while number < FREE and ready < (len(events) if number == FREE - 1 else SECOND):
            gate = prepare(ready, gate)
            ready += 1
    new_weights = jax.ShapeDtypeStruct((count * rows, wide), jnp.bfloat16)
    new_one = new_two = jax.ShapeDtypeStruct((rows, wide), jnp.float32)
    top = jnp.zeros((), jnp.int32)
    ones, twos = [], []
    for c in range(CHUNKS):
        grad = moving[c]
        if c:
            grad, moving[c - 1] = lax.optimization_barrier((grad, moving[c - 1]))
        one = beta_one * moment_one[:, cols[c]] + (1.0 - beta_one) * grad
        two = beta_two * moment_two[:, cols[c]] + (1.0 - beta_two) * grad * grad
        first = one / (1.0 - beta_one**adam_step)
        second = two / (1.0 - beta_two**adam_step)
        update = learn_rate * (
            first / (jnp.sqrt(second) + epsilon) + weight_decay * master[:, cols[c]]
        )
        moving[c] = straight((master[:, cols[c]] - update).astype(jnp.bfloat16))
        ones.append(straight(one))
        twos.append(straight(two))
    waiting = collections.deque()

    def put(into):
        c, step, piece = waiting.popleft()
        at = owners[-turns[c] * step % count]
        return place(into, piece, at * rows, starts[c])

    for step in range(count):
        for c, turn in enumerate(turns):
            waiting.append((c, step, moving[c]))
            if len(waiting) > LAG:
                new_weights = put(new_weights)
            if step < count - 1:
                if step or c >= LAG:
                    moving[c], new_weights = lax.optimization_barrier((moving[c], new_weights))
                moving[c] = lax.ppermute(moving[c], "dp", pairs[turn])
        for c in range(CHUNKS):
            if SPREAD[c] == step:
                new_one = place(new_one, ones[c], top, starts[c])
                new_two = place(new_two, twos[c], top, starts[c])
                new_weights, new_one, new_two = lax.optimization_barrier(
                    (new_weights, new_one, new_two)
                )
    while waiting:
        new_weights = put(new_weights)
    return (new_weights, new_one, new_two)


def solution(mesh):
    return jax.shard_map(
        shards,
        mesh=mesh,
        in_specs=(
            P("dp", "tensor"),
            P("dp", None),
            P("dp"),
            P(),
            P("dp", "tensor"),
            P("dp", "tensor"),
            P("dp", "tensor"),
        ),
        out_specs=(P(None, "tensor"), P("dp", "tensor"), P("dp", "tensor")),
        check_vma=False,
    )
```
